768 devices in a mesh: rows: 32 (over x, y), groups: 24 (over z, core).
Axes of the slice: x: 4, y: 8, z: 12, core: 2. Of those that a mesh axis runs over, the one named last changes fastest.
Arguments:
- next_owner: int32 [98304, 16, 1], P(('rows', 'groups')), may hold values from 0 to 31; in each aligned block of 2048 rows (0 to 2047, 2048 to 4095, ..., all dimensions but the last counted through in order) at most 96 rows name the same one
- next_row: int32 [98304, 16], P(('rows', 'groups')), may hold values from 0 to 767
- prev_owner: int32 [98304, 16, 1], P(('rows', 'groups')), may hold values from 0 to 31; in each aligned block of 2048 rows (0 to 2047, 2048 to 4095, ..., all dimensions but the last counted through in order) at most 96 rows name the same one
- prev_row: int32 [98304, 16], P(('rows', 'groups')), may hold values from 0 to 767
- emb_now: bfloat16 [98304, 4096], P(('rows', 'groups')), may hold values from -6 to 6
- prev_grad: bfloat16 [98304, 4096], P(('rows', 'groups')), may hold values from -6 to 6
- labels: int32 [98304], P(('rows', 'groups')), may hold values 0 or 1
- emb_table: float32 [24576, 256], P('rows'), may hold values from -6 to 6
- row_accum: float32 [24576], P('rows'), may hold values from 0.1 to 10
- proj_in: bfloat16 [128, 4096], replicated, may hold values from -0.09375 to 0.09375
- proj_out: bfloat16 [128, 4096], replicated, may hold values from -0.5 to 0.5
- cross_bias: float32 [4096], replicated, may hold values from -3 to 3
- head_weight: bfloat16 [4096], replicated, may hold values from -0.09375 to 0.09375
Outputs:
- next_emb: bfloat16 [98304, 4096], P(('rows', 'groups'))
- emb_grad: bfloat16 [98304, 4096], P(('rows', 'groups'))
- new_table: float32 [24576, 256], P('rows')
- new_accum: float32 [24576], P('rows')
- grad_in: float32 [128, 4096], P(None, 'rows')
- grad_out: float32 [128, 4096], P(None, 'rows')
- grad_bias: float32 [4096], P('rows')
- grad_head: float32 [4096], P('rows')
The draws below stay inside these ranges and needn't reach their ends.
Inputs may be any that keep to these rules, and one draw needn't show every extreme that they name: `next_owner`: at most 96 of the 2048 lookups of one device's samples name rows held by one device of the rows axis, and exactly 96 for some devices. `prev_owner`: at most 96 of the 2048 lookups of one device's samples name rows held by one device of the rows axis, and exactly 96 for some devices.
All inputs are finite; a program needn't handle non-finite values. No bound on the sum of `labels` on one device may be relied on, other than what follows from the above.
Results may differ from the reference program's by a relative error of at most 0.0059.
Values may be sent and summed in bfloat16 or wider, within the bound.
A program may use at most 64 MiB of HBM per device.

```python
import math
import jax
import jax.numpy as jnp
import numpy as np
from jax import lax

E = 256
F = 16
R = 128
ROWS_DEV = 768
D = 4096
LOOK_DEV = 2048
CAP = 96
BATCH = 98304
VOCAB = 24576
N_ROWS = 32
N_GROUPS = 24


def set_ends(values, key, least, top_value):
    longest = values.shape.index(max(values.shape))
    spots = []
    for shift in (0, 1):
        where = [jax.random.randint(jax.random.fold_in(key, axis), (), 0, length) for axis, length in enumerate(values.shape)]
        where[longest] = (where[longest] + shift) % values.shape[longest]
        spots.append(tuple(where))
    return values.at[spots[0]].set(least).at[spots[1]].set(top_value)


def level_of(stream_key, dims, cuts, least, top_value):
    factor_of = 1.0
    for axis_at, parts in cuts:
        draws = jax.random.uniform(jax.random.fold_in(jax.random.fold_in(stream_key, 6), axis_at), (parts,), jnp.float32, least / len(cuts), top_value / len(cuts))
        factor_of = factor_of * jnp.repeat(jnp.exp(draws), dims[axis_at] // parts).reshape((-1,) + (1,) * (len(dims) - 1 - axis_at))
    return factor_of


def rank_bounds(number_of, slope):
    loads = [(1 << 20) // math.isqrt(grade ** slope) + 1 for grade in range(1, number_of + 1)]
    spread = 1 + sum(loads) // (1 << 30)
    return np.cumsum(np.array([max(1, weight // spread) for weight in loads]))


def ranked_ids(stream_key, extent, count, skew):
    listing = rank_bounds(count, skew)
    pick = jax.random.randint(jax.random.fold_in(stream_key, 1), extent, 0, int(listing[count - 1]))
    rank = jnp.searchsorted(jnp.asarray(listing, jnp.int32), pick, side="right")
    return jax.random.permutation(jax.random.fold_in(stream_key, 2), count)[rank].astype(jnp.int32)


def routed_block(rng, own, number, rows, amount, top, most, slope):
    sequence = jax.random.permutation(rng, amount)
    crowded, common = portions_of(amount, rows * top, most, slope, True), portions_of(amount, rows * top, most, slope, False)
    places = jnp.arange(amount)

    def named(sizes, rotation):
        used = int((sizes > 0).sum())
        fixed = max(1, used // 4)
        moved = fixed + (places - fixed + rotation * (used - fixed)) % max(1, amount - fixed)
        return jnp.zeros((amount,), jnp.int32).at[sequence[jnp.where(places < fixed, places, moved)]].set(jnp.asarray(sizes, jnp.int32))

    sizes = jnp.where(number % 4 == 0, named(crowded, number // 4), named(common, number - number // 4 - 1))
    mixed = jax.random.permutation(jax.random.fold_in(own, 3), amount)
    donor, receiver = mixed[0:amount // 2 * 2:2], mixed[1:amount // 2 * 2:2]
    margin = jnp.minimum(sizes[donor] - 1, most - sizes[receiver]) // 2
    margin = jnp.where((donor == sequence[0]) | (receiver == sequence[0]) | (sizes[receiver] == 0), 0, jnp.maximum(margin, 0))
    moved = jax.random.randint(jax.random.fold_in(own, 4), (amount // 2,), 0, 1 << 20) % (margin + 1)
    sizes = sizes.at[donor].add(-moved).at[receiver].add(moved)
    members = jnp.searchsorted(jnp.cumsum(sizes), jnp.arange(rows * top), side="right").astype(jnp.int32)
    table = members.reshape(top, rows).T
    table = table[jax.random.permutation(jax.random.fold_in(own, 1), rows)]
    rotation = jax.random.randint(jax.random.fold_in(own, 2), (rows, 1), 0, top)
    return jnp.take_along_axis(table, (jnp.arange(top)[None, :] + rotation) % top, axis=1)


def portions_of(amount, total, bound, slope, full):
    loads = [(1 << 20) // math.isqrt(rank ** slope) + 1 for rank in range(1, amount + 1)]
    largest = bound if full else min(bound, max(-(-total // amount), total * loads[0] // sum(loads)))
    least = 1 if total - largest >= amount - 1 else 0
    counts, spare = [largest] + [least] * (amount - 1), total - largest - least * (amount - 1)
    while spare > 0:
        movable = [i for i in range(1, amount) if counts[i] < largest] or [i for i in range(1, amount) if counts[i] < bound]
        pool, budget = sum([loads[i] for i in movable]), spare
        for i in movable:
            addition = min(bound - counts[i], max(1, budget * loads[i] // pool), spare)
            counts[i] = counts[i] + addition
            spare = spare - addition
    return np.array(counts)


def scatter_about(own_key, dims, width, reach, cuts=(), dtype=jnp.bfloat16):
    level = level_of(own_key, dims, cuts, -0.22, 0.18) if cuts else 1.0
    values = jax.random.normal(own_key, dims, jnp.float32) * width * level
    return jnp.minimum(jnp.maximum(values, -reach), reach).astype(dtype)


def setup_inputs(seed: int = 0) -> dict:
    streams_of = jax.random.split(jax.random.key(seed), 14)
    next_owner_keys = jax.random.split(jax.random.fold_in(streams_of[0], 1), BATCH * F // LOOK_DEV)
    next_owner_turns = jax.random.permutation(jax.random.fold_in(streams_of[0], 3), BATCH * F // LOOK_DEV)
    next_owner = jax.vmap(lambda own, number: routed_block(jax.random.fold_in(streams_of[0], 2), own, number, LOOK_DEV, N_ROWS, 1, CAP, 2))(next_owner_keys, next_owner_turns).reshape((BATCH, F, 1))
    next_row = set_ends(ranked_ids(streams_of[1], (BATCH, F), ROWS_DEV, 2), jax.random.fold_in(streams_of[1], 3), 0, ROWS_DEV - 1).astype(jnp.int32)
    prev_owner_keys = jax.random.split(jax.random.fold_in(streams_of[2], 1), BATCH * F // LOOK_DEV)
    prev_owner_turns = jax.random.permutation(jax.random.fold_in(streams_of[2], 3), BATCH * F // LOOK_DEV)
    prev_owner = jax.vmap(lambda own, number: routed_block(jax.random.fold_in(streams_of[2], 2), own, number, LOOK_DEV, N_ROWS, 1, CAP, 2))(prev_owner_keys, prev_owner_turns).reshape((BATCH, F, 1))
    prev_row = set_ends(ranked_ids(streams_of[3], (BATCH, F), ROWS_DEV, 2), jax.random.fold_in(streams_of[3], 3), 0, ROWS_DEV - 1).astype(jnp.int32)
    emb_now = scatter_about(streams_of[4], (BATCH, D), 1.0, 6.0, ((0, 768),))
    prev_grad = scatter_about(streams_of[5], (BATCH, D), 1.0, 6.0, ((0, 768),))
    labels = set_ends((jax.random.randint(streams_of[6], (BATCH,), 0, 2) < 1).astype(jnp.int32), jax.random.fold_in(streams_of[6], 1), 0, 1)
    emb_table = scatter_about(streams_of[7], (VOCAB, E), 1.0, 6.0, ((0, 32),), jnp.float32)
    row_accum = jnp.clip(jnp.exp(math.log(10.0) - 4.6051702 * jax.random.uniform(streams_of[8], (VOCAB,), jnp.float32) ** level_of(streams_of[8], (VOCAB,), ((0, 32),), -0.2, 0.2)), 0.1, 10.0)
    proj_in = scatter_about(streams_of[9], (R, D), D ** -0.5, 0.09375)
    proj_out = scatter_about(streams_of[10], (R, D), R ** -0.5, 0.5)
    cross_bias = scatter_about(streams_of[11], (D,), 0.5, 3.0, (), jnp.float32)
    head_weight = scatter_about(streams_of[12], (D,), D ** -0.5, 0.09375)
    return dict(next_owner=next_owner, next_row=next_row, prev_owner=prev_owner, prev_row=prev_row, emb_now=emb_now, prev_grad=prev_grad, labels=labels, emb_table=emb_table, row_accum=row_accum, proj_in=proj_in, proj_out=proj_out, cross_bias=cross_bias, head_weight=head_weight)


LEARN_RATE = 0.1
EPSILON = 1e-06
LOSS_SCALE = 64.0

def reference(next_owner, next_row, prev_owner, prev_row, emb_now, prev_grad, labels, emb_table, row_accum, proj_in, proj_out, cross_bias, head_weight):
    table_half = emb_table.astype(jnp.bfloat16)
    next_ids = next_owner[:, :, 0] * ROWS_DEV + next_row
    next_emb = table_half[next_ids].reshape(BATCH, D)
    head_float = head_weight.astype(jnp.float32)

    def dense_step(totals, pieces):
        emb_block, label_block = pieces
        latent = jnp.dot(emb_block, proj_in.T, preferred_element_type=jnp.float32).astype(jnp.bfloat16)
        cross_gate = jnp.dot(latent, proj_out, preferred_element_type=jnp.float32) + cross_bias
        inputs = emb_block.astype(jnp.float32)
        crossed = inputs * cross_gate + inputs
        logits = lax.optimization_barrier(jnp.sum(crossed * head_float[None, :], axis=1))
        errors = LOSS_SCALE * (jax.nn.sigmoid(logits) - label_block.astype(jnp.float32))
        grad_crossed = errors[:, None] * head_float[None, :]
        grad_gate = (grad_crossed * inputs).astype(jnp.bfloat16)
        grad_latent = jnp.dot(grad_gate, proj_out.T, preferred_element_type=jnp.float32).astype(jnp.bfloat16)
        emb_grad = (grad_crossed * (cross_gate + 1.0) + jnp.dot(grad_latent, proj_in, preferred_element_type=jnp.float32)).astype(jnp.bfloat16)
        grad_in = jnp.dot(grad_latent.T, emb_block, preferred_element_type=jnp.float32)
        grad_out = jnp.dot(latent.T, grad_gate, preferred_element_type=jnp.float32)
        grad_bias = lax.optimization_barrier(jnp.sum(grad_gate.astype(jnp.float32), axis=0))
        grad_head = lax.optimization_barrier(jnp.sum(errors[:, None] * crossed, axis=0))
        totals = (totals[0] + grad_in, totals[1] + grad_out, totals[2] + grad_bias, totals[3] + grad_head)
        return (totals, emb_grad)
    start = (jnp.zeros((R, D), jnp.float32), jnp.zeros((R, D), jnp.float32), jnp.zeros((D,), jnp.float32), jnp.zeros((D,), jnp.float32))
    totals, grad_blocks = lax.scan(dense_step, start, (emb_now.reshape(N_GROUPS, -1, D), labels.reshape(N_GROUPS, -1)))
    emb_grad = grad_blocks.reshape(BATCH, D)
    factor = 1.0 / math.sqrt(BATCH)
    prev_ids = (prev_owner[:, :, 0] * ROWS_DEV + prev_row).reshape(N_GROUPS, -1)
    grad_pieces = prev_grad.reshape(N_GROUPS, -1, E)

    def row_step(total_rows, pieces):
        id_block, block_grad = pieces
        return (total_rows.at[id_block].add(block_grad.astype(jnp.float32)), None)
    row_sums, unused = lax.scan(row_step, jnp.zeros((VOCAB, E), jnp.float32), (prev_ids, grad_pieces))
    new_accum = row_accum + lax.optimization_barrier(jnp.mean(row_sums * row_sums, axis=1))
    new_table = emb_table - LEARN_RATE * row_sums / (jnp.sqrt(new_accum)[:, None] + EPSILON)
    return (next_emb, emb_grad, new_table, new_accum, totals[0] * factor, totals[1] * factor, totals[2] * factor, totals[3] * factor)
```

```python
import math

import jax
import jax.numpy as jnp
from jax import lax
from jax.sharding import PartitionSpec as P

LEARN_RATE = 0.1
EPSILON = 1e-06
LOSS_SCALE = 64.0


def slot_keys(owners, peer_count, capacity):
    blocks, width = owners.shape
    onehot = (owners[:, :, None] == jnp.arange(peer_count, dtype=jnp.int32)).astype(jnp.bfloat16)
    earlier = jnp.tril(jnp.ones((width, width), jnp.bfloat16), -1)
    within = jnp.einsum("ij,bjp->bip", earlier, onehot, preferred_element_type=jnp.float32)
    totals = jnp.sum(onehot.astype(jnp.float32), axis=1)
    offsets = jnp.cumsum(totals, axis=0) - totals
    ranks = jnp.sum((within + offsets[:, None, :]) * onehot.astype(jnp.float32), axis=2)
    return owners * capacity + ranks.astype(jnp.int32)


def exchange(values, axis):
    return lax.all_to_all(values, axis, split_axis=0, concat_axis=0, tiled=True)


def shards(
    next_owner,
    next_row,
    prev_owner,
    prev_row,
    emb_now,
    prev_grad,
    labels,
    emb_table,
    row_accum,
    proj_in,
    proj_out,
    cross_bias,
    head_weight,
):
    peers = lax.axis_size("rows")
    copies = lax.axis_size("groups")
    samples, columns = emb_now.shape
    shard_rows, row_width = emb_table.shape
    features = next_owner.shape[1]
    lookups = samples * features
    capacity = 3 * lookups // (2 * peers)
    slots = peers * capacity
    rank = proj_in.shape[0]
    part = columns // peers
    batch_total = samples * peers * copies
    half = jnp.bfloat16
    full = jnp.float32

    next_key = slot_keys(next_owner[:, :, 0].T, peers, capacity)
    prev_key = slot_keys(prev_owner[:, :, 0].T, peers, capacity)
    slot_ids = jnp.arange(slots, dtype=jnp.int32)
    next_pick = (slot_ids[:, None] == next_key.reshape(1, lookups)).astype(half)
    prev_pick = (slot_ids[:, None] == prev_key.reshape(1, lookups)).astype(half)

    def asks(pick, rows):
        flat = rows.T.reshape(lookups) + 1
        digits = jnp.stack([flat // 32, flat % 32], axis=1).astype(half)
        found = jnp.dot(pick, digits, preferred_element_type=full)
        return (found[:, 0] * 32 + found[:, 1]).astype(jnp.int32) - 1

    asked = exchange(
        jnp.concatenate(
            [asks(next_pick, next_row).reshape(peers, capacity), asks(prev_pick, prev_row).reshape(peers, capacity)],
            axis=1,
        ),
        "rows",
    )
    next_asked = asked[:, :capacity].reshape(slots)
    prev_asked = asked[:, capacity:].reshape(slots)
    grads = prev_grad.reshape(samples, features, row_width).transpose(1, 0, 2).reshape(lookups, row_width)
    outgoing = jnp.dot(prev_pick, grads, preferred_element_type=full).astype(half)
    arrived = exchange(outgoing.reshape(peers, capacity, row_width), "rows").reshape(slots, row_width)

    head_float = head_weight.astype(full)
    latent = lax.dot_general(emb_now, proj_in, (((1,), (1,)), ((), ())), preferred_element_type=full).astype(half)
    cross_gate = jnp.dot(latent, proj_out, preferred_element_type=full) + cross_bias
    inputs = emb_now.astype(full)
    crossed = inputs * cross_gate + inputs
    logits = jnp.sum(crossed * head_float[None, :], axis=1)
    errors = LOSS_SCALE * (jax.nn.sigmoid(logits) - labels.astype(full))
    grad_crossed = errors[:, None] * head_float[None, :]
    grad_gate = (grad_crossed * inputs).astype(half)
    grad_latent = lax.dot_general(
        grad_gate, proj_out, (((1,), (1,)), ((), ())), preferred_element_type=full
    ).astype(half)
    emb_grad = (
        grad_crossed * (cross_gate + 1.0) + jnp.dot(grad_latent, proj_in, preferred_element_type=full)
    ).astype(half)
    grad_in = lax.dot_general(grad_latent, emb_now, (((0,), (0,)), ((), ())), preferred_element_type=full)
    grad_out = lax.dot_general(latent, grad_gate, (((0,), (0,)), ((), ())), preferred_element_type=full)
    grad_bias = jnp.sum(grad_gate.astype(full), axis=0)
    grad_head = jnp.sum(errors[:, None] * crossed, axis=0)
    dense_rows = 2 * rank + 2
    padded = -(-dense_rows // (2 * copies)) * 2 * copies
    dense = jnp.concatenate(
        [grad_in, grad_out, grad_bias[None], grad_head[None], jnp.zeros((padded - dense_rows, columns), full)], axis=0
    ).astype(half)
    dense = dense.reshape(padded, peers, part).transpose(1, 0, 2)
    dense = jnp.sum(exchange(dense, "rows").astype(full), axis=0)

    table_half = emb_table.astype(half)
    row_ids = jnp.arange(shard_rows, dtype=jnp.int32)
    fetched = jnp.dot(
        (next_asked[:, None] == row_ids[None, :]).astype(half), table_half, preferred_element_type=full
    ).astype(half)
    looked = exchange(fetched.reshape(peers, capacity, row_width), "rows").reshape(slots, row_width)
    next_emb = lax.dot_general(
        next_pick, looked, (((0,), (0,)), ((), ())), preferred_element_type=full
    ).astype(half)
    next_emb = next_emb.reshape(features, samples, row_width).transpose(1, 0, 2).reshape(samples, columns)

    shard_grad = jnp.dot(
        (row_ids[:, None] == prev_asked[None, :]).astype(half), arrived, preferred_element_type=full
    )
    share = shard_rows // copies
    pieces = jnp.concatenate(
        [
            shard_grad.reshape(copies, share, row_width),
            dense.reshape(copies, padded // (2 * copies), 2 * part),
        ],
        axis=1,
    ).astype(half)
    mine = jnp.sum(exchange(pieces, "groups").astype(full), axis=0).astype(half)
    whole = exchange(jnp.broadcast_to(mine[None], (copies,) + mine.shape), "groups").astype(full)
    row_sums = whole[:, :share].reshape(shard_rows, row_width)
    totals = whole[:, share:].reshape(padded, part) * (1.0 / math.sqrt(batch_total))
    new_accum = row_accum + jnp.mean(row_sums * row_sums, axis=1)
    new_table = emb_table - LEARN_RATE * row_sums / (jnp.sqrt(new_accum)[:, None] + EPSILON)
    return (
        next_emb,
        emb_grad,
        new_table,
        new_accum,
        totals[:rank],
        totals[rank : 2 * rank],
        totals[2 * rank],
        totals[2 * rank + 1],
    )


def solution(mesh):
    placed = (
        P(("rows", "groups"), None, None),
        P(("rows", "groups"), None),
        P(("rows", "groups"), None, None),
        P(("rows", "groups"), None),
        P(("rows", "groups"), None),
        P(("rows", "groups"), None),
        P(("rows", "groups")),
        P("rows", None),
        P("rows"),
        P(),
        P(),
        P(),
        P(),
    )
    return jax.shard_map(
        shards,
        mesh=mesh,
        in_specs=placed,
        out_specs=(
            P(("rows", "groups"), None),
            P(("rows", "groups"), None),
            P("rows", None),
            P("rows"),
            P(None, "rows"),
            P(None, "rows"),
            P("rows"),
            P("rows"),
        ),
        check_vma=False,
    )
```
